32 devices in a mesh: rep: 8 (over z, y), shard: 4 (over x, core).
Axes of the slice: x: 2, y: 2, z: 4, core: 2. Of those that a mesh axis runs over, the one named last changes fastest.
Arguments:
- hidden_in: bfloat16 [4096, 960], P(('rep', 'shard')), may hold values from -6 to 6
- segment_ids: int32 [4096], P(('rep', 'shard')), may hold values from 0 to 31, as said below
- positions: int32 [4096], P(('rep', 'shard')), may hold values from 0 to 511, as said below
- norm_attn: bfloat16 [960], P('shard'), may hold values from 0.5 to 1.5
- w_query: bfloat16 [960, 960], P('shard'), may hold values from -0.19364917 to 0.19364917
- w_key: bfloat16 [960, 320], P('shard'), may hold values from -0.19364917 to 0.19364917
- w_value: bfloat16 [960, 320], P('shard'), may hold values from -0.1875 to 0.1875
- w_out: bfloat16 [960, 960], P('shard'), may hold values from -1.5 to 1.5
- norm_mlp: bfloat16 [960], P('shard'), may hold values from 0.29882812 to 3
- w_gate: bfloat16 [960, 2560], P('shard'), may hold values from -0.1875 to 0.1875
- w_up: bfloat16 [960, 2560], P('shard'), may hold values from -0.1875 to 0.1875
- w_down: bfloat16 [2560, 960], P('shard'), may hold values from -0.25 to 0.25
- grad_out: bfloat16 [4096, 960], P(('rep', 'shard')), may hold values from -6 to 6
Outputs:
- output: bfloat16 [4096, 960], P(('rep', 'shard'))
- grad_hidden: float32 [4096, 960], P(('rep', 'shard'))
- grad_norm_attn: float32 [960], P('shard')
- grad_w_query: float32 [960, 960], P('shard')
- grad_w_key: float32 [960, 320], P('shard')
- grad_w_value: float32 [960, 320], P('shard')
- grad_w_out: float32 [960, 960], P('shard')
- grad_norm_mlp: float32 [960], P('shard')
- grad_w_gate: float32 [960, 2560], P('shard')
- grad_w_up: float32 [960, 2560], P('shard')
- grad_w_down: float32 [2560, 960], P('shard')
The draws below stay inside these ranges and needn't reach their ends.
Inputs may be any that keep to these rules, and one draw needn't show every extreme that they name: `segment_ids`: within each row of 512 consecutive tokens the ids never fall, and no two rows share an id. Within a segment positions rise by one from token to token; the first segment of a row may begin above 0, every other begins at 0.
All inputs are finite; a program needn't handle non-finite values.
Results may differ from the reference program's by a relative error of at most 0.019.
Values may be sent and summed in bfloat16 or wider, within the bound.
A program may use at most 192 MiB of HBM per device.

```python
import math
import jax
import jax.numpy as jnp
from jax import lax

D = 960
H = 15
KV = 5
HD = 64
FF = 2560
TOK_DEV = 128
TOKENS = 4096
N_REP = 8
N_SHARD = 4


def segment_layout(key):
    row_len = TOK_DEV * N_SHARD
    boundary = jax.random.randint(jax.random.fold_in(key, 11), (N_REP, 3), 1, row_len)
    first_end = jnp.min(boundary, axis=1, keepdims=True)
    offsets = jax.random.randint(jax.random.fold_in(key, 12), (N_REP, 1), 0, row_len - first_end + 1)
    row_base = jnp.arange(N_REP, dtype=jnp.int32)[:, None]
    offsets = jnp.where(row_base == 0, row_len - first_end, offsets)
    token_idx = jnp.arange(row_len, dtype=jnp.int32)
    passed = boundary[:, None, :] <= token_idx[None, :, None]
    segment = jnp.sum(passed.astype(jnp.int32), axis=-1)
    doc_start = jnp.max(jnp.where(passed, boundary[:, None, :], 0), axis=-1)
    seg_ids = segment + 4 * row_base
    places = token_idx[None, :] - doc_start + jnp.where(segment == 0, offsets, 0)
    return (seg_ids.reshape(-1).astype(jnp.int32), places.reshape(-1).astype(jnp.int32))


def draw_segment_ids(key, part):
    return segment_layout(key)[0]


def draw_positions(key, part):
    return segment_layout(key)[1]


def draw_w_query(key, part):
    factor = D ** (-0.5)
    query = jnp.clip(jax.random.normal(jax.random.fold_in(key, 21), (D, H * HD), jnp.float32), -6.0, 6.0) * factor
    return query.astype(jnp.bfloat16)


def draw_w_key(key, part):
    factor = D ** (-0.5)
    keys = jnp.clip(jax.random.normal(jax.random.fold_in(key, 22), (D, KV * HD), jnp.float32), -6.0, 6.0) * factor
    return keys.astype(jnp.bfloat16)


def block_scale(key, shape, split, low, top_value):
    level, own = 1.0, jax.random.fold_in(key, 6)
    for position, blocks in split:
        heights = jnp.exp(jax.random.uniform(jax.random.fold_in(own, position), (blocks,), jnp.float32, low / len(split), top_value / len(split)))
        level = level * jnp.repeat(heights, shape[position] // blocks).reshape([-1 if axis == position else 1 for axis in range(len(shape))])
    return level


def normal_values(own_key, dims, deviation, bound, shards=(), held_as=jnp.bfloat16):
    level = block_scale(own_key, dims, shards, -0.22, 0.18) if shards else 1.0
    values = jax.random.normal(own_key, dims, jnp.float32) * deviation * level
    return jnp.minimum(jnp.maximum(values, -bound), bound).astype(held_as)


def setup_inputs(seed: int = 0) -> dict:
    key_list = jax.random.split(jax.random.key(seed), 14)
    return {
        "hidden_in": normal_values(key_list[0], (TOKENS, D), 1.0, 6.0, ((0, 32),)),
        "segment_ids": draw_segment_ids(jax.random.fold_in(key_list[13], 71), 0),
        "positions": draw_positions(jax.random.fold_in(key_list[13], 71), 0),
        "norm_attn": jnp.clip(1.0 + 0.1 * jax.random.normal(key_list[3], (D,), jnp.float32), 0.5, 1.5).astype(jnp.bfloat16),
        "w_query": draw_w_query(jax.random.fold_in(key_list[13], 71), 0),
        "w_key": draw_w_key(jax.random.fold_in(key_list[13], 71), 0),
        "w_value": normal_values(key_list[6], (D, KV * HD), D ** -0.5, 0.1875, ((0, 4),)),
        "w_out": normal_values(key_list[7], (H * HD, D), (H * HD // 64) ** -0.5, 1.5, ((0, 4),)),
        "norm_mlp": jnp.clip(jnp.exp(math.log(3.0) - 2.306499 * jax.random.uniform(key_list[8], (D,), jnp.float32) ** block_scale(key_list[8], (D,), ((0, 4),), -0.2, 0.2)), 0.29882812, 3.0).astype(jnp.bfloat16),
        "w_gate": normal_values(key_list[9], (D, FF), D ** -0.5, 0.1875, ((0, 4),)),
        "w_up": normal_values(key_list[10], (D, FF), D ** -0.5, 0.1875, ((0, 4),)),
        "w_down": normal_values(key_list[11], (FF, D), (FF // 4) ** -0.5, 0.25, ((0, 4),)),
        "grad_out": normal_values(key_list[12], (TOKENS, D), 1.0, 6.0, ((0, 32),)),
    }


EPS = 1e-05
THETA = 100000.0
NEG = -1e+30

def rope_tables(positions, head_size):
    half_size = head_size // 2
    frequency = THETA ** (-(jnp.arange(half_size, dtype=jnp.float32) * 2.0 / head_size))
    angles = positions.astype(jnp.float32)[:, None] * frequency[None, :]
    return (jnp.cos(angles), jnp.sin(angles))

def rotate(values, cosine, sine, direction):
    half_size = values.shape[-1] // 2
    first_half = values[..., :half_size]
    second_half = values[..., half_size:]
    cos_table = cosine[:, None, :]
    sin_table = sine[:, None, :] * direction
    return jnp.concatenate([first_half * cos_table - second_half * sin_table, second_half * cos_table + first_half * sin_table], axis=-1)

def norm_forward(values, gain):
    inverse = lax.rsqrt(lax.optimization_barrier(jnp.mean(values * values, axis=-1, keepdims=True)) + EPS)
    return (values * inverse * gain, inverse)

def norm_backward(values, inverse, gain, upstream):
    scaled = upstream * gain
    grad_gain = lax.optimization_barrier(jnp.sum(upstream * values * inverse, axis=0))
    inner = lax.optimization_barrier(jnp.mean(scaled * values, axis=-1, keepdims=True))
    return (inverse * scaled - values * inverse * inverse * inverse * inner, grad_gain)

def rounded(values):
    return lax.optimization_barrier(values.astype(jnp.bfloat16)).astype(jnp.float32)

def allowed_mask(query_seg, query_idx, key_seg, key_idx):
    return (query_seg[:, None] == key_seg[None, :]) & (key_idx[None, :] <= query_idx[:, None])

def attention_forward(query_b, key_b, value_b, row_seg):
    length, heads_kv, head_size = key_b.shape
    block_rows = min(length, 512)
    score_scale = 1.0 / math.sqrt(head_size)
    query4 = query_b.reshape(length, heads_kv, -1, head_size)
    token_idx = jnp.arange(length, dtype=jnp.int32)
    keys32 = key_b.astype(jnp.float32)
    values32 = value_b.astype(jnp.float32)

    def one_block(number):
        first = number * block_rows
        queries = lax.dynamic_slice_in_dim(query4, first, block_rows, 0).astype(jnp.float32)
        seg_rows = lax.dynamic_slice_in_dim(row_seg, first, block_rows, 0)
        idx_rows = first + jnp.arange(block_rows, dtype=jnp.int32)
        allowed = allowed_mask(seg_rows, idx_rows, row_seg, token_idx)[:, None, None, :]
        scores = jnp.einsum('tgrd,jgd->tgrj', queries, keys32) * score_scale
        scores = jnp.where(allowed, scores, NEG)
        row_max = lax.optimization_barrier(jnp.max(scores, axis=-1))
        row_sum = lax.optimization_barrier(jnp.sum(jnp.where(allowed, jnp.exp(scores - row_max[..., None]), 0.0), axis=-1))
        log_total = row_max + jnp.log(row_sum)
        weights = jnp.where(allowed, jnp.exp(scores - log_total[..., None]), 0.0)
        result = jnp.einsum('tgrj,jgd->tgrd', weights, values32)
        return (result.astype(jnp.bfloat16).reshape(block_rows, -1), log_total)
    outputs, totals = lax.map(one_block, jnp.arange(length // block_rows, dtype=jnp.int32))
    return (outputs.reshape(length, -1), totals.reshape(length, heads_kv, -1))

def attention_backward(query_b, key_b, value_b, row_seg, attn_b, log_total, grad_attn_b):
    length, heads_kv, head_size = key_b.shape
    block_rows = min(length, 512)
    score_scale = 1.0 / math.sqrt(head_size)
    query4 = query_b.reshape(length, heads_kv, -1, head_size).astype(jnp.float32)
    grad4 = grad_attn_b.reshape(length, heads_kv, -1, head_size).astype(jnp.float32)
    attn4 = attn_b.reshape(length, heads_kv, -1, head_size).astype(jnp.float32)
    delta = lax.optimization_barrier(jnp.sum(grad4 * attn4, axis=-1))
    token_idx = jnp.arange(length, dtype=jnp.int32)
    keys32 = key_b.astype(jnp.float32)
    values32 = value_b.astype(jnp.float32)

    def one_block(carry, number):
        grad_keys, grad_values = carry
        first = number * block_rows
        queries = lax.dynamic_slice_in_dim(query4, first, block_rows, 0)
        grad_rows = lax.dynamic_slice_in_dim(grad4, first, block_rows, 0)
        delta_rows = lax.dynamic_slice_in_dim(delta, first, block_rows, 0)
        total_rows = lax.dynamic_slice_in_dim(log_total, first, block_rows, 0)
        seg_rows = lax.dynamic_slice_in_dim(row_seg, first, block_rows, 0)
        idx_rows = first + jnp.arange(block_rows, dtype=jnp.int32)
        allowed = allowed_mask(seg_rows, idx_rows, row_seg, token_idx)[:, None, None, :]
        scores = jnp.einsum('tgrd,jgd->tgrj', queries, keys32) * score_scale
        scores = jnp.where(allowed, scores, NEG)
        probs = jnp.where(allowed, jnp.exp(scores - total_rows[..., None]), 0.0)
        grad_values = grad_values + jnp.einsum('tgrj,tgrd->jgd', rounded(probs), grad_rows)
        grad_probs = jnp.einsum('tgrd,jgd->tgrj', grad_rows, values32)
        grad_scores = rounded(probs * (grad_probs - delta_rows[..., None]))
        grad_query = jnp.einsum('tgrj,jgd->tgrd', grad_scores, keys32) * score_scale
        grad_keys = grad_keys + jnp.einsum('tgrj,tgrd->jgd', grad_scores, queries) * score_scale
        return ((grad_keys, grad_values), grad_query)
    zeros_kv = jnp.zeros((length, heads_kv, head_size), jnp.float32)
    (grad_keys, grad_values), grad_query = lax.scan(one_block, (zeros_kv, zeros_kv), jnp.arange(length // block_rows, dtype=jnp.int32))
    return (grad_query.reshape(length, -1, head_size), grad_keys, grad_values)

def reference(hidden_in, segment_ids, positions, norm_attn, w_query, w_key, w_value, w_out, norm_mlp, w_gate, w_up, w_down, grad_out):
    row_len = TOK_DEV * N_SHARD
    gain_attn = norm_attn.astype(jnp.float32)
    gain_mlp = norm_mlp.astype(jnp.float32)

    def one_row(sums, inputs):
        row_in, row_seg, row_pos, row_grad = inputs
        resid = row_in.astype(jnp.float32)
        normed, inv_attn = norm_forward(resid, gain_attn)
        normed_b = normed.astype(jnp.bfloat16)
        cos_table, sin_table = rope_tables(row_pos, HD)
        query = jnp.dot(normed_b, w_query, preferred_element_type=jnp.float32).reshape(row_len, H, HD)
        query_b = rotate(query, cos_table, sin_table, 1.0).astype(jnp.bfloat16)
        keys = jnp.dot(normed_b, w_key, preferred_element_type=jnp.float32).reshape(row_len, KV, HD)
        key_b = rotate(keys, cos_table, sin_table, 1.0).astype(jnp.bfloat16)
        value_b = jnp.dot(normed_b, w_value, preferred_element_type=jnp.float32).astype(jnp.bfloat16).reshape(row_len, KV, HD)
        attn_b, log_total = attention_forward(query_b, key_b, value_b, row_seg)
        mixed = resid + jnp.dot(attn_b, w_out, preferred_element_type=jnp.float32)
        normed_mlp, inv_mlp = norm_forward(mixed, gain_mlp)
        normed_mlp_b = normed_mlp.astype(jnp.bfloat16)
        gate = jnp.dot(normed_mlp_b, w_gate, preferred_element_type=jnp.float32)
        upper = jnp.dot(normed_mlp_b, w_up, preferred_element_type=jnp.float32)
        sigma = jax.nn.sigmoid(gate)
        act_b = (gate * sigma * upper).astype(jnp.bfloat16)
        result = (mixed + jnp.dot(act_b, w_down, preferred_element_type=jnp.float32)).astype(jnp.bfloat16)
        grad_w_down = jnp.dot(act_b.T, row_grad, preferred_element_type=jnp.float32)
        grad_act = jnp.dot(row_grad, w_down.T, preferred_element_type=jnp.float32)
        grad_gate_b = (grad_act * upper * sigma * (1.0 + gate * (1.0 - sigma))).astype(jnp.bfloat16)
        grad_up_b = (grad_act * gate * sigma).astype(jnp.bfloat16)
        grad_w_gate = jnp.dot(normed_mlp_b.T, grad_gate_b, preferred_element_type=jnp.float32)
        grad_w_up = jnp.dot(normed_mlp_b.T, grad_up_b, preferred_element_type=jnp.float32)
        grad_normed_mlp = jnp.dot(grad_gate_b, w_gate.T, preferred_element_type=jnp.float32) + jnp.dot(grad_up_b, w_up.T, preferred_element_type=jnp.float32)
        grad_mixed_n, grad_gain_mlp = norm_backward(mixed, inv_mlp, gain_mlp, grad_normed_mlp)
        grad_mixed = row_grad.astype(jnp.float32) + grad_mixed_n
        grad_mixed_b = grad_mixed.astype(jnp.bfloat16)
        grad_w_out = jnp.dot(attn_b.T, grad_mixed_b, preferred_element_type=jnp.float32)
        grad_attn_b = jnp.dot(grad_mixed_b, w_out.T, preferred_element_type=jnp.float32).astype(jnp.bfloat16)
        grad_query, grad_keys, grad_values = attention_backward(query_b, key_b, value_b, row_seg, attn_b, log_total, grad_attn_b)
        grad_query_b = rotate(grad_query, cos_table, sin_table, -1.0).astype(jnp.bfloat16).reshape(row_len, H * HD)
        grad_key_b = rotate(grad_keys, cos_table, sin_table, -1.0).astype(jnp.bfloat16).reshape(row_len, KV * HD)
        grad_value_b = grad_values.astype(jnp.bfloat16).reshape(row_len, KV * HD)
        grad_w_query = jnp.dot(normed_b.T, grad_query_b, preferred_element_type=jnp.float32)
        grad_w_key = jnp.dot(normed_b.T, grad_key_b, preferred_element_type=jnp.float32)
        grad_w_value = jnp.dot(normed_b.T, grad_value_b, preferred_element_type=jnp.float32)
        grad_normed = jnp.dot(grad_query_b, w_query.T, preferred_element_type=jnp.float32)
        grad_normed = grad_normed + jnp.dot(grad_key_b, w_key.T, preferred_element_type=jnp.float32)
        grad_normed = grad_normed + jnp.dot(grad_value_b, w_value.T, preferred_element_type=jnp.float32)
        grad_resid_n, grad_gain_attn = norm_backward(resid, inv_attn, gain_attn, grad_normed)
        grad_input = grad_mixed + grad_resid_n
        terms = (grad_gain_attn, grad_w_query, grad_w_key, grad_w_value, grad_w_out, grad_gain_mlp, grad_w_gate, grad_w_up, grad_w_down)
        new_sums = tuple((total + term for total, term in zip(sums, terms)))
        return (new_sums, (result, grad_input))
    zeros = tuple((jnp.zeros(weight.shape, jnp.float32) for weight in (norm_attn, w_query, w_key, w_value, w_out, norm_mlp, w_gate, w_up, w_down)))
    inputs = (hidden_in.reshape(N_REP, row_len, D), segment_ids.reshape(N_REP, row_len), positions.reshape(N_REP, row_len), grad_out.reshape(N_REP, row_len, D))
    sums, (results, grad_inputs) = lax.scan(one_row, zeros, inputs)
    return (results.reshape(TOKENS, D), grad_inputs.reshape(TOKENS, D), sums[0], sums[1], sums[2], sums[3], sums[4], sums[5], sums[6], sums[7], sums[8])
```

```python
import functools
import math

import jax
import jax.numpy as jnp
from jax import lax
from jax.experimental import pallas as pl
from jax.experimental.pallas import tpu as pltpu
from jax.sharding import PartitionSpec as P

H = 15
KV = 5
HD = 64

EPS = 1e-05
THETA = 100000.0
NEG = -1e30
MESH = pl.DeviceIdType.MESH
BF = jnp.bfloat16
F32 = jnp.float32


def rope_tables(positions, head_size):
    half_size = head_size // 2
    frequency = THETA ** (-(jnp.arange(half_size, dtype=F32) * 2.0 / head_size))
    angles = positions.astype(F32)[:, None] * frequency[None, :]
    return (jnp.cos(angles), jnp.sin(angles))


def rotate(values, cosine, sine, direction):
    half_size = values.shape[-1] // 2
    first_half = values[..., :half_size]
    second_half = values[..., half_size:]
    cos_table = cosine[:, None, :]
    sin_table = sine[:, None, :] * direction
    return jnp.concatenate(
        [
            first_half * cos_table - second_half * sin_table,
            second_half * cos_table + first_half * sin_table,
        ],
        axis=-1,
    )


def norm_forward(values, gain):
    inverse = lax.rsqrt(jnp.mean(values * values, axis=-1, keepdims=True) + EPS)
    return (values * inverse * gain, inverse)


def norm_backward(values, inverse, gain, upstream):
    scaled = upstream * gain
    grad_gain = jnp.sum(upstream * values * inverse, axis=0)
    inner = jnp.mean(scaled * values, axis=-1, keepdims=True)
    return (inverse * scaled - values * inverse * inverse * inverse * inner, grad_gain)


def dot(a, b):
    return jnp.dot(a, b, preferred_element_type=F32)


def exchange_kernel(n, n_gather, n_scatter, *refs):
    total = n_gather + n_scatter
    ins, outs = refs[:total], refs[total : 2 * total]
    local_sem, send_sem, recv_sem = refs[2 * total :]
    me = lax.axis_index("shard")
    chips = n // 2
    chip, core = me // 2, me % 2
    mate = 2 * chip + (1 - core)

    barrier = pltpu.get_barrier_semaphore()
    for d in range(1, n):
        pl.semaphore_signal(
            barrier, inc=1, device_id={"shard": (me + d) % n}, device_id_type=MESH
        )
    pl.semaphore_wait(barrier, n - 1)

    count = [0]

    def remote(src, dst, to):
        i = count[0]
        count[0] += 1
        copy = pltpu.make_async_remote_copy(
            src_ref=src,
            dst_ref=dst,
            send_sem=send_sem.at[i],
            recv_sem=recv_sem.at[i],
            device_id={"shard": to},
            device_id_type=MESH,
        )
        copy.start()
        return copy

    pending = []
    far = []
    for a in range(n_gather):
        for k in range(1, chips):
            peer = 2 * ((chip + k) % chips) + core
            far.append((a, k, remote(ins[a], outs[a].at[me], peer)))
    for a in range(n_gather, total):
        for d in range(1, n):
            peer = (me + d) % n
            pending.append(remote(ins[a].at[peer], outs[a].at[me], peer))
    for a in range(n_gather):
        pending.append(remote(ins[a], outs[a].at[me], mate))
    own = []
    for a in range(total):
        src = ins[a] if a < n_gather else ins[a].at[me]
        copy = pltpu.make_async_copy(src, outs[a].at[me], local_sem.at[a])
        copy.start()
        own.append(copy)
    for a, k, copy in far:
        copy.wait_recv()
        origin = 2 * ((chip + chips - k) % chips) + core
        pending.append(remote(outs[a].at[origin], outs[a].at[origin], mate))
    for _, _, copy in far:
        copy.wait_send()
    for copy in pending:
        copy.wait()
    for copy in own:
        copy.wait()


def exchange(n, cid, gathers, scatters):
    chips = n // 2
    g, s = len(gathers), len(scatters)
    copies = g * (2 * (chips - 1) + 1) + s * (n - 1)
    shapes = [jax.ShapeDtypeStruct((n,) + a.shape, a.dtype) for a in gathers]
    shapes += [jax.ShapeDtypeStruct(a.shape, a.dtype) for a in scatters]
    out = pl.pallas_call(
        functools.partial(exchange_kernel, n, g, s),
        out_shape=shapes,
        in_specs=[pl.BlockSpec(memory_space=pl.ANY)] * (g + s),
        out_specs=[pl.BlockSpec(memory_space=pl.ANY)] * (g + s),
        scratch_shapes=[
            pltpu.SemaphoreType.DMA((g + s,)),
            pltpu.SemaphoreType.DMA((copies,)),
            pltpu.SemaphoreType.DMA((copies,)),
        ],
        compiler_params=pltpu.CompilerParams(collective_id=cid, has_side_effects=True),
    )(*gathers, *scatters)
    return out[:g], out[g:]


def rep_sum_kernel(zs, n, *refs):
    ins, outs = refs[:n], refs[n : 2 * n]
    near, sums, others = refs[2 * n : 3 * n], refs[3 * n : 4 * n], refs[4 * n : 5 * n]
    send_sem, recv_sem = refs[5 * n :]
    me = lax.axis_index("rep")
    side, place = me % 2, me // 2
    partner = 2 * place + (1 - side)

    barrier = pltpu.get_barrier_semaphore()
    pl.semaphore_signal(barrier, inc=1, device_id={"rep": partner}, device_id_type=MESH)
    for k in range(1, zs):
        peer = 2 * ((place + k) % zs) + side
        pl.semaphore_signal(barrier, inc=1, device_id={"rep": peer}, device_id_type=MESH)
    pl.semaphore_wait(barrier, zs)

    count = [0]

    def remote(src, dst, to):
        i = count[0]
        count[0] += 1
        copy = pltpu.make_async_remote_copy(
            src_ref=src,
            dst_ref=dst,
            send_sem=send_sem.at[i],
            recv_sem=recv_sem.at[i],
            device_id={"rep": to},
            device_id_type=MESH,
        )
        copy.start()
        return copy

    sends = []
    first = [remote(ins[a].at[1 - side], near[a], partner) for a in range(n)]
    second, third, fourth = {}, {}, {}

    def pair_sum(a):
        first[a].wait_recv()

        def body(z, carry):
            sums[a][z] = (ins[a][side, z].astype(F32) + near[a][z].astype(F32)).astype(BF)
            return carry

        lax.fori_loop(0, zs, body, 0)
        second[a] = []
        for k in range(1, zs):
            at = (place + k) % zs
            second[a].append(remote(sums[a].at[at], others[a].at[k - 1], 2 * at + side))

    def line_sum(a):
        for copy in second[a]:
            copy.wait_recv()
        value = sums[a][place].astype(F32)
        for k in range(1, zs):
            value = value + others[a][k - 1].astype(F32)
        outs[a][side, place] = value.astype(BF)
        third[a] = []
        for k in range(1, zs):
            at = (place + k) % zs
            block = outs[a].at[side, place]
            third[a].append(remote(block, block, 2 * at + side))

    def share(a):
        for copy in third[a]:
            copy.wait_recv()
        fourth[a] = remote(outs[a].at[side], outs[a].at[side], partner)

    for t in range(n + 2):
        if t < n:
            pair_sum(t)
        if 0 <= t - 1 < n:
            line_sum(t - 1)
        if 0 <= t - 2 < n:
            share(t - 2)
    for a in range(n):
        first[a].wait_send()
        for copy in second[a]:
            copy.wait_send()
        for copy in third[a]:
            copy.wait_send()
        fourth[a].wait()


def rep_sum(reps, cid, arrays):
    zs = reps // 2
    n = len(arrays)
    blocks = [a.reshape(2, zs, a.shape[0] // reps, a.shape[1]) for a in arrays]
    copies = n * (2 + 2 * (zs - 1))
    out = pl.pallas_call(
        functools.partial(rep_sum_kernel, zs, n),
        out_shape=[jax.ShapeDtypeStruct(b.shape, b.dtype) for b in blocks],
        in_specs=[pl.BlockSpec(memory_space=pltpu.VMEM)] * n,
        out_specs=[pl.BlockSpec(memory_space=pltpu.VMEM)] * n,
        scratch_shapes=[pltpu.VMEM(b.shape[1:], BF) for b in blocks]
        + [pltpu.VMEM(b.shape[1:], BF) for b in blocks]
        + [pltpu.VMEM((zs - 1,) + b.shape[2:], BF) for b in blocks]
        + [pltpu.SemaphoreType.DMA((copies,)), pltpu.SemaphoreType.DMA((copies,))],
        compiler_params=pltpu.CompilerParams(
            collective_id=cid, has_side_effects=True, vmem_limit_bytes=44 * 1024 * 1024
        ),
    )(*blocks)
    return [o.reshape(a.shape) for o, a in zip(out, arrays)]


def local(
    n,
    reps,
    hidden_in,
    segment_ids,
    positions,
    norm_attn,
    w_query,
    w_key,
    w_value,
    w_out,
    norm_mlp,
    w_gate,
    w_up,
    w_down,
    grad_out,
):
    tok_rows, width = hidden_in.shape
    row_len = tok_rows * n
    first_row = lax.axis_index("shard") * tok_rows
    groups = H // KV
    score_scale = 1.0 / math.sqrt(HD)
    query_idx = first_row + jnp.arange(tok_rows, dtype=jnp.int32)

    gains = jnp.pad(jnp.stack([norm_attn, norm_mlp]), ((0, 14), (0, 0)))
    seg8 = jnp.broadcast_to(segment_ids[None, :], (8, tok_rows))
    got, _ = exchange(
        n, 0, [seg8, gains, w_query, w_key, w_value, w_out, w_gate, w_up, w_down], []
    )
    row_segments = got[0][:, 0, :].reshape(row_len)
    gain_attn = got[1][:, 0, :].reshape(width).astype(F32)
    gain_mlp = got[1][:, 1, :].reshape(width).astype(F32)
    wq, wk, wv, wo, wg, wu, wd = [w.reshape(-1, w.shape[-1]) for w in got[2:]]

    key_idx = jnp.arange(row_len, dtype=jnp.int32)
    allowed = (
        (segment_ids[:, None] == row_segments[None, :])
        & (key_idx[None, :] <= query_idx[:, None])
    )[:, None, None, :]

    resid = hidden_in.astype(F32)
    normed, inv_attn = norm_forward(resid, gain_attn)
    normed_b = normed.astype(BF)
    cos_table, sin_table = rope_tables(positions, HD)
    query = dot(normed_b, wq).reshape(tok_rows, H, HD)
    query_b = rotate(query, cos_table, sin_table, 1.0).astype(BF)
    keys = dot(normed_b, wk).reshape(tok_rows, KV, HD)
    key_b = rotate(keys, cos_table, sin_table, 1.0).astype(BF)
    value_b = dot(normed_b, wv).astype(BF)
    query4 = query_b.reshape(tok_rows, KV, groups, HD)
    (kv_row,), _ = exchange(
        n, 1, [jnp.concatenate([key_b.reshape(tok_rows, KV * HD), value_b], axis=1)], []
    )
    kv_row = kv_row.reshape(row_len, 2, KV, HD)
    key_row, value_row = kv_row[:, 0], kv_row[:, 1]

    scores = (
        jnp.einsum("tgrd,jgd->tgrj", query4, key_row, preferred_element_type=F32) * score_scale
    )
    scores = jnp.where(allowed, scores, NEG)
    row_max = jnp.max(scores, axis=-1)
    weights = jnp.where(allowed, jnp.exp(scores - row_max[..., None]), 0.0)
    row_sum = jnp.sum(weights, axis=-1)
    probs = weights / row_sum[..., None]
    probs_b = probs.astype(BF)
    accum = jnp.einsum("tgrj,jgd->tgrd", probs_b, value_row, preferred_element_type=F32)
    attn4 = accum.astype(BF)
    attn_b = attn4.reshape(tok_rows, H * HD)
    mixed = resid + dot(attn_b, wo)
    normed_mlp, inv_mlp = norm_forward(mixed, gain_mlp)
    normed_mlp_b = normed_mlp.astype(BF)
    gate = dot(normed_mlp_b, wg)
    upper = dot(normed_mlp_b, wu)
    sigma = jax.nn.sigmoid(gate)
    act_b = (gate * sigma * upper).astype(BF)
    result = (mixed + dot(act_b, wd)).astype(BF)

    grad_act = dot(grad_out, wd.T)
    grad_gate_b = (grad_act * upper * sigma * (1.0 + gate * (1.0 - sigma))).astype(BF)
    grad_up_b = (grad_act * gate * sigma).astype(BF)
    grad_normed_mlp = dot(grad_gate_b, wg.T) + dot(grad_up_b, wu.T)
    grad_mixed_n, grad_gain_mlp = norm_backward(mixed, inv_mlp, gain_mlp, grad_normed_mlp)
    grad_mixed = grad_out.astype(F32) + grad_mixed_n
    grad_mixed_b = grad_mixed.astype(BF)
    grad_attn_b = dot(grad_mixed_b, wo.T).astype(BF)
    grad_attn4 = grad_attn_b.reshape(tok_rows, KV, groups, HD)
    delta = jnp.sum(grad_attn4.astype(F32) * attn4.astype(F32), axis=-1)

    value_part = jnp.einsum("tgrj,tgrd->jgd", probs_b, grad_attn4, preferred_element_type=F32)
    grad_probs = jnp.einsum("tgrd,jgd->tgrj", grad_attn4, value_row, preferred_element_type=F32)
    grad_scores = (probs * (grad_probs - delta[..., None])).astype(BF)
    grad_query = (
        jnp.einsum("tgrj,jgd->tgrd", grad_scores, key_row, preferred_element_type=F32)
        * score_scale
    )
    key_part = (
        jnp.einsum("tgrj,tgrd->jgd", grad_scores, query4, preferred_element_type=F32)
        * score_scale
    )
    parts = jnp.concatenate(
        [key_part.reshape(row_len, KV * HD), value_part.reshape(row_len, KV * HD)], axis=1
    )
    _, (parts,) = exchange(n, 2, [], [parts.astype(BF).reshape(n, tok_rows, 2 * KV * HD)])
    own = jnp.sum(parts.astype(F32), axis=0)
    own_keys = own[:, : KV * HD].reshape(tok_rows, KV, HD)
    grad_query_b = (
        rotate(grad_query.reshape(tok_rows, H, HD), cos_table, sin_table, -1.0)
        .astype(BF)
        .reshape(tok_rows, H * HD)
    )
    grad_key_b = (
        rotate(own_keys, cos_table, sin_table, -1.0).astype(BF).reshape(tok_rows, KV * HD)
    )
    grad_value_b = own[:, KV * HD :].astype(BF)
    grad_normed = dot(grad_query_b, wq.T) + dot(grad_key_b, wk.T) + dot(grad_value_b, wv.T)
    grad_resid_n, grad_gain_attn = norm_backward(resid, inv_attn, gain_attn, grad_normed)
    grad_hidden = grad_mixed + grad_resid_n

    gain_sums = lax.psum(jnp.stack([grad_gain_attn, grad_gain_mlp]), ("rep", "shard"))
    rows = width // n
    gain_own = lax.dynamic_slice_in_dim(gain_sums, lax.axis_index("shard") * rows, rows, 1)

    def sliced(x):
        return x.reshape(tok_rows, n, -1).transpose(1, 0, 2)

    right_small = jnp.concatenate([grad_query_b, grad_key_b, grad_value_b, grad_mixed_b], axis=1)
    (g_gate, g_up, g_small, g_out), (x_attn, x_ctx, x_mlp, x_act) = exchange(
        n,
        3,
        [grad_gate_b, grad_up_b, right_small, grad_out],
        [sliced(normed_b), sliced(attn_b), sliced(normed_mlp_b), sliced(act_b)],
    )

    def padded(x):
        size = x.shape[-1]
        full = -(-size // (16 * reps)) * (16 * reps)
        return jnp.pad(x.reshape(row_len, size), ((0, 0), (0, full - size)))

    def product(x, g):
        return dot(padded(x).T, g.reshape(row_len, -1)).astype(BF)

    g_small = g_small.reshape(row_len, -1)
    cut = H * HD + 2 * KV * HD
    small = jnp.concatenate(
        [product(x_attn, g_small[:, :cut]), product(x_ctx, g_small[:, cut:])], axis=1
    )
    t_gate, t_up, t_small, t_down = rep_sum(
        reps, 4, [product(x_mlp, g_gate), product(x_mlp, g_up), small, product(x_act, g_out)]
    )
    t_small = t_small[:rows].astype(F32)
    q, k = H * HD, KV * HD
    return (
        result,
        grad_hidden,
        gain_own[0],
        t_small[:, :q],
        t_small[:, q : q + k],
        t_small[:, q + k : q + 2 * k],
        t_small[:, q + 2 * k :],
        gain_own[1],
        t_gate[:rows].astype(F32),
        t_up[:rows].astype(F32),
        t_down[: w_down.shape[0]].astype(F32),
    )


def solution(mesh):
    both = P(("rep", "shard"), None)
    tokens = P(("rep", "shard"))
    vector = P("shard")
    matrix = P("shard", None)
    return jax.shard_map(
        functools.partial(local, mesh.shape["shard"], mesh.shape["rep"]),
        mesh=mesh,
        in_specs=(both, tokens, tokens, vector, matrix, matrix, matrix, matrix, vector)
        + (matrix, matrix, matrix, both),
        out_specs=(both, both, vector, matrix, matrix, matrix, matrix, vector)
        + (matrix, matrix, matrix),
        check_vma=False,
    )
```

```python
import functools
import math

import jax
import jax.numpy as jnp
from jax import lax
from jax.experimental import pallas as pl
from jax.experimental.pallas import tpu as pltpu
from jax.sharding import PartitionSpec as P

H = 15
KV = 5
HD = 64

EPS = 1e-05
THETA = 100000.0
NEG = -1e30
MESH = pl.DeviceIdType.MESH
BF = jnp.bfloat16
F32 = jnp.float32


def rope_tables(positions, head_size):
    half_size = head_size // 2
    frequency = THETA ** (-(jnp.arange(half_size, dtype=F32) * 2.0 / head_size))
    angles = positions.astype(F32)[:, None] * frequency[None, :]
    return (jnp.cos(angles), jnp.sin(angles))


def rotate(values, cosine, sine, direction):
    half_size = values.shape[-1] // 2
    first_half = values[..., :half_size]
    second_half = values[..., half_size:]
    cos_table = cosine[:, None, :]
    sin_table = sine[:, None, :] * direction
    return jnp.concatenate(
        [
            first_half * cos_table - second_half * sin_table,
            second_half * cos_table + first_half * sin_table,
        ],
        axis=-1,
    )


def norm_forward(values, gain):
    inverse = lax.rsqrt(jnp.mean(values * values, axis=-1, keepdims=True) + EPS)
    return (values * inverse * gain, inverse)


def norm_backward(values, inverse, gain, upstream):
    scaled = upstream * gain
    grad_gain = jnp.sum(upstream * values * inverse, axis=0)
    inner = jnp.mean(scaled * values, axis=-1, keepdims=True)
    return (inverse * scaled - values * inverse * inverse * inverse * inner, grad_gain)


def dot(a, b):
    return jnp.dot(a, b, preferred_element_type=F32)


def exchange_kernel(n, n_gather, n_scatter, *refs):
    total = n_gather + n_scatter
    ins, outs = refs[:total], refs[total : 2 * total]
    local_sem, send_sem, recv_sem = refs[2 * total :]
    me = lax.axis_index("shard")
    chips = n // 2
    chip, core = me // 2, me % 2
    mate = 2 * chip + (1 - core)

    barrier = pltpu.get_barrier_semaphore()
    for d in range(1, n):
        pl.semaphore_signal(
            barrier, inc=1, device_id={"shard": (me + d) % n}, device_id_type=MESH
        )
    pl.semaphore_wait(barrier, n - 1)

    count = [0]

    def remote(src, dst, to):
        i = count[0]
        count[0] += 1
        copy = pltpu.make_async_remote_copy(
            src_ref=src,
            dst_ref=dst,
            send_sem=send_sem.at[i],
            recv_sem=recv_sem.at[i],
            device_id={"shard": to},
            device_id_type=MESH,
        )
        copy.start()
        return copy

    pending = []
    far = []
    for a in range(n_gather):
        for k in range(1, chips):
            peer = 2 * ((chip + k) % chips) + core
            far.append((a, k, remote(ins[a], outs[a].at[me], peer)))
    for a in range(n_gather, total):
        for d in range(1, n):
            peer = (me + d) % n
            pending.append(remote(ins[a].at[peer], outs[a].at[me], peer))
    for a in range(n_gather):
        pending.append(remote(ins[a], outs[a].at[me], mate))
    own = []
    for a in range(total):
        src = ins[a] if a < n_gather else ins[a].at[me]
        copy = pltpu.make_async_copy(src, outs[a].at[me], local_sem.at[a])
        copy.start()
        own.append(copy)
    for a, k, copy in far:
        copy.wait_recv()
        origin = 2 * ((chip + chips - k) % chips) + core
        pending.append(remote(outs[a].at[origin], outs[a].at[origin], mate))
    for _, _, copy in far:
        copy.wait_send()
    for copy in pending:
        copy.wait()
    for copy in own:
        copy.wait()


def exchange(n, cid, gathers, scatters):
    chips = n // 2
    g, s = len(gathers), len(scatters)
    copies = g * (2 * (chips - 1) + 1) + s * (n - 1)
    shapes = [jax.ShapeDtypeStruct((n,) + a.shape, a.dtype) for a in gathers]
    shapes += [jax.ShapeDtypeStruct(a.shape, a.dtype) for a in scatters]
    out = pl.pallas_call(
        functools.partial(exchange_kernel, n, g, s),
        out_shape=shapes,
        in_specs=[pl.BlockSpec(memory_space=pl.ANY)] * (g + s),
        out_specs=[pl.BlockSpec(memory_space=pl.ANY)] * (g + s),
        scratch_shapes=[
            pltpu.SemaphoreType.DMA((g + s,)),
            pltpu.SemaphoreType.DMA((copies,)),
            pltpu.SemaphoreType.DMA((copies,)),
        ],
        compiler_params=pltpu.CompilerParams(collective_id=cid, has_side_effects=True),
    )(*gathers, *scatters)
    return out[:g], out[g:]


def weight_kernel(n, n_small, axes, *refs):
    n_big = len(axes)
    total = n_small + n_big
    ins, outs = refs[:total], refs[total : 2 * total]
    local_sem, send_sem, recv_sem = refs[2 * total :]
    me, rep = lax.axis_index("shard"), lax.axis_index("rep")
    chips = n // 2
    chip, core = me // 2, me % 2
    mate = {"shard": 2 * chip + (1 - core)}
    near_a = {"rep": rep + 1 - 2 * (rep % 2)}
    near_b = {"rep": rep + 2 - 4 * ((rep // 2) % 2)}
    own_q = rep % 4
    quarter_b, quarter_d = (own_q + 2) % 4, 3 - own_q
    quarter_a = own_q + 1 - 2 * (own_q % 2)

    barrier = pltpu.get_barrier_semaphore()
    for d in range(1, n):
        pl.semaphore_signal(
            barrier, inc=1, device_id={"shard": (me + d) % n}, device_id_type=MESH
        )
    for there in (near_a, near_b):
        pl.semaphore_signal(barrier, inc=1, device_id=there, device_id_type=MESH)
    pl.semaphore_wait(barrier, n + 1)

    count = [0]

    def remote(src, dst, to):
        i = count[0]
        count[0] += 1
        copy = pltpu.make_async_remote_copy(
            src_ref=src,
            dst_ref=dst,
            send_sem=send_sem.at[i],
            recv_sem=recv_sem.at[i],
            device_id=to,
            device_id_type=MESH,
        )
        copy.start()
        return copy

    def piece(ref, a, which, part=None):
        axis = axes[a - n_small]
        unit = 16 if axis == 0 else 128
        size = ins[a].shape[axis] // 4
        lo = (size // unit) * 2 // 5 * unit
        first, length = {None: (0, size), 0: (0, lo), 1: (lo, size - lo)}[part]
        at = pl.ds(pl.multiple_of(which * size + first, unit), length)
        return ref.at[at, :] if axis == 0 else ref.at[:, at]

    waits = []
    received = []

    def to_mate(ref):
        waits.append(remote(ref, ref, mate))

    def arrived(copy):
        copy.wait_recv()
        received.append(copy)

    direct, side_a, side_b, corner_x, corner_a, plain = {}, {}, {}, {}, {}, []
    for a in range(n_small):
        for k in range(1, chips):
            peer = {"shard": 2 * ((chip + k) % chips) + core}
            plain.append((a, k, remote(ins[a], outs[a].at[me], peer)))
        waits.append(remote(ins[a], outs[a].at[me], mate))
    for a in range(n_small, total):
        for k in range(1, chips):
            peer = {"shard": 2 * ((chip + k) % chips) + core}
            direct[a, k] = remote(
                piece(ins[a], a, own_q), piece(outs[a].at[me], a, own_q), peer
            )
    for a in range(n_small, total):
        for k in range(1, chips):
            peer = {"shard": 2 * ((chip + k) % chips) + core}
            corner_x[a, k] = remote(
                piece(ins[a], a, quarter_d, 0), piece(outs[a].at[me], a, quarter_d, 0), peer
            )
        waits.append(remote(ins[a], outs[a].at[me], mate))
    own = []
    for a in range(total):
        copy = pltpu.make_async_copy(ins[a], outs[a].at[me], local_sem.at[a])
        copy.start()
        own.append(copy)

    def origin(k):
        return 2 * ((chip + chips - k) % chips) + core

    def spread(a):
        for k in range(1, chips):
            arrived(direct[a, k])
            block = piece(outs[a].at[origin(k)], a, own_q)
            side_a[a, k] = remote(block, block, near_a)
            side_b[a, k] = remote(block, block, near_b)
            to_mate(block)

    def pass_on(a):
        for k in range(1, chips):
            arrived(side_b[a, k])
            slot = outs[a].at[origin(k)]
            block = piece(slot, a, quarter_b, 1)
            corner_a[a, k] = remote(block, block, near_a)
            to_mate(piece(slot, a, quarter_b))
            arrived(side_a[a, k])
            to_mate(piece(slot, a, quarter_a))

    def finish(a):
        for k in range(1, chips):
            slot = outs[a].at[origin(k)]
            arrived(corner_x[a, k])
            to_mate(piece(slot, a, quarter_d, 0))
            arrived(corner_a[a, k])
            to_mate(piece(slot, a, quarter_d, 1))

    for t in range(n_big + 2):
        if t < n_big:
            spread(n_small + t)
        if 0 <= t - 1 < n_big:
            pass_on(n_small + t - 1)
        if 0 <= t - 2 < n_big:
            finish(n_small + t - 2)
    for a, k, copy in plain:
        arrived(copy)
        to_mate(outs[a].at[origin(k)])
    for copy in received:
        copy.wait_send()
    for copy in waits:
        copy.wait()
    for copy in own:
        copy.wait()


def gather_weights(n, cid, small, big):
    arrays = list(small) + [a for a, _ in big]
    chips = n // 2
    copies = len(small) * (2 * chips - 1) + len(big) * (10 * (chips - 1) + 1)
    total = len(arrays)
    return pl.pallas_call(
        functools.partial(weight_kernel, n, len(small), tuple(axis for _, axis in big)),
        out_shape=[jax.ShapeDtypeStruct((n,) + a.shape, a.dtype) for a in arrays],
        in_specs=[pl.BlockSpec(memory_space=pl.ANY)] * total,
        out_specs=[pl.BlockSpec(memory_space=pl.ANY)] * total,
        scratch_shapes=[
            pltpu.SemaphoreType.DMA((total,)),
            pltpu.SemaphoreType.DMA((copies,)),
            pltpu.SemaphoreType.DMA((copies,)),
        ],
        compiler_params=pltpu.CompilerParams(collective_id=cid, has_side_effects=True),
    )(*arrays)


def rep_sum_kernel(zs, n, *refs):
    gain_in, refs = refs[0], refs[1:]
    ins, gain_out, refs = refs[:n], refs[n], refs[n + 1 :]
    outs, near, sums = refs[:n], refs[n : 2 * n], refs[2 * n : 3 * n]
    others = refs[3 * n : 4 * n]
    gain_near, gain_pair, gain_all, send_sem, recv_sem = refs[4 * n :]
    me = lax.axis_index("rep")
    side, place = me % 2, me // 2
    partner = 2 * place + (1 - side)

    barrier = pltpu.get_barrier_semaphore()
    pl.semaphore_signal(barrier, inc=1, device_id={"rep": partner}, device_id_type=MESH)
    for k in range(1, zs):
        peer = 2 * ((place + k) % zs) + side
        pl.semaphore_signal(barrier, inc=1, device_id={"rep": peer}, device_id_type=MESH)
    pl.semaphore_wait(barrier, zs)

    count = [0]

    def remote(src, dst, to):
        i = count[0]
        count[0] += 1
        copy = pltpu.make_async_remote_copy(
            src_ref=src,
            dst_ref=dst,
            send_sem=send_sem.at[i],
            recv_sem=recv_sem.at[i],
            device_id={"rep": to},
            device_id_type=MESH,
        )
        copy.start()
        return copy

    gain_first = remote(gain_in, gain_near, partner)
    first = [remote(ins[a].at[1 - side], near[a], partner) for a in range(n)]
    second, third, fourth = {}, {}, {}
    gain_first.wait_recv()
    gain_pair[...] = gain_in[...] + gain_near[...]
    gain_all[place] = gain_pair[...]
    gain_second = [
        remote(gain_pair, gain_all.at[place], 2 * ((place + k) % zs) + side)
        for k in range(1, zs)
    ]

    def pair_sum(a):
        first[a].wait_recv()

        def body(z, carry):
            sums[a][z] = (ins[a][side, z].astype(F32) + near[a][z].astype(F32)).astype(BF)
            return carry

        lax.fori_loop(0, zs, body, 0)
        second[a] = []
        for k in range(1, zs):
            at = (place + k) % zs
            second[a].append(remote(sums[a].at[at], others[a].at[k - 1], 2 * at + side))

    def line_sum(a):
        for copy in second[a]:
            copy.wait_recv()
        value = sums[a][place].astype(F32)
        for k in range(1, zs):
            value = value + others[a][k - 1].astype(F32)
        outs[a][side, place] = value.astype(BF)
        third[a] = []
        for k in range(1, zs):
            at = (place + k) % zs
            block = outs[a].at[side, place]
            third[a].append(remote(block, block, 2 * at + side))

    def share(a):
        for copy in third[a]:
            copy.wait_recv()
        fourth[a] = remote(outs[a].at[side], outs[a].at[side], partner)

    for t in range(n + 2):
        if t < n:
            pair_sum(t)
        if 0 <= t - 1 < n:
            line_sum(t - 1)
        if 0 <= t - 2 < n:
            share(t - 2)
    for copy in gain_second:
        copy.wait()
    value = gain_all[0]
    for z in range(1, zs):
        value = value + gain_all[z]
    gain_out[...] = value
    gain_first.wait_send()
    for a in range(n):
        first[a].wait_send()
        for copy in second[a]:
            copy.wait_send()
        for copy in third[a]:
            copy.wait_send()
        fourth[a].wait()


def rep_sum(reps, cid, gain, arrays):
    zs = reps // 2
    n = len(arrays)
    blocks = [a.reshape(2, zs, a.shape[0] // reps, a.shape[1]) for a in arrays]
    copies = n * (2 + 2 * (zs - 1)) + zs
    out = pl.pallas_call(
        functools.partial(rep_sum_kernel, zs, n),
        out_shape=[jax.ShapeDtypeStruct(b.shape, b.dtype) for b in [gain] + blocks],
        in_specs=[pl.BlockSpec(memory_space=pltpu.VMEM)] * (n + 1),
        out_specs=[pl.BlockSpec(memory_space=pltpu.VMEM)] * (n + 1),
        scratch_shapes=[pltpu.VMEM(b.shape[1:], BF) for b in blocks]
        + [pltpu.VMEM(b.shape[1:], BF) for b in blocks]
        + [pltpu.VMEM((zs - 1,) + b.shape[2:], BF) for b in blocks]
        + [pltpu.VMEM(gain.shape, F32)] * 2
        + [pltpu.VMEM((zs,) + gain.shape, F32)]
        + [pltpu.SemaphoreType.DMA((copies,)), pltpu.SemaphoreType.DMA((copies,))],
        compiler_params=pltpu.CompilerParams(
            collective_id=cid, has_side_effects=True, vmem_limit_bytes=44 * 1024 * 1024
        ),
    )(gain, *blocks)
    return out[0], [o.reshape(a.shape) for o, a in zip(out[1:], arrays)]


def local(
    n,
    reps,
    hidden_in,
    segment_ids,
    positions,
    norm_attn,
    w_query,
    w_key,
    w_value,
    w_out,
    norm_mlp,
    w_gate,
    w_up,
    w_down,
    grad_out,
):
    tok_rows, width = hidden_in.shape
    row_len = tok_rows * n
    first_row = lax.axis_index("shard") * tok_rows
    groups = H // KV
    score_scale = 1.0 / math.sqrt(HD)
    query_idx = first_row + jnp.arange(tok_rows, dtype=jnp.int32)

    gains = jnp.pad(jnp.stack([norm_attn, norm_mlp]), ((0, 14), (0, 0)))
    seg8 = jnp.broadcast_to(segment_ids[None, :], (8, tok_rows))
    rows = width // n

    def row_pad(x, unit):
        return jnp.pad(x, ((0, -x.shape[0] % unit), (0, 0)))

    w_small = jnp.concatenate([w_query, w_key, w_value, w_out], axis=1)
    got = gather_weights(
        n,
        0,
        [seg8, gains],
        [
            (row_pad(w_small, 16), 1),
            (row_pad(w_gate, 16), 1),
            (row_pad(w_up, 16), 1),
            (row_pad(w_down, 64), 0),
        ],
    )
    row_segments = got[0][:, 0, :].reshape(row_len)
    gain_attn = got[1][:, 0, :].reshape(width).astype(F32)
    gain_mlp = got[1][:, 1, :].reshape(width).astype(F32)
    ws, wg, wu = [w[:, :rows].reshape(width, -1) for w in got[2:5]]
    wd = got[5][:, : w_down.shape[0]].reshape(-1, width)
    q, k = H * HD, KV * HD
    cut = q + 2 * k
    wqkv, wo = ws[:, :cut], ws[:, cut:]

    key_idx = jnp.arange(row_len, dtype=jnp.int32)
    allowed = (
        (segment_ids[:, None] == row_segments[None, :])
        & (key_idx[None, :] <= query_idx[:, None])
    )[:, None, None, :]

    resid = hidden_in.astype(F32)
    normed, inv_attn = norm_forward(resid, gain_attn)
    normed_b = normed.astype(BF)
    cos_table, sin_table = rope_tables(positions, HD)
    qkv = dot(normed_b, wqkv)
    query = qkv[:, :q].reshape(tok_rows, H, HD)
    query_b = rotate(query, cos_table, sin_table, 1.0).astype(BF)
    keys = qkv[:, q : q + k].reshape(tok_rows, KV, HD)
    key_b = rotate(keys, cos_table, sin_table, 1.0).astype(BF)
    value_b = qkv[:, q + k :].astype(BF)
    query4 = query_b.reshape(tok_rows, KV, groups, HD)
    (kv_row,), _ = exchange(
        n, 1, [jnp.concatenate([key_b.reshape(tok_rows, KV * HD), value_b], axis=1)], []
    )
    kv_row = kv_row.reshape(row_len, 2, KV, HD)
    key_row, value_row = kv_row[:, 0], kv_row[:, 1]

    scores = (
        jnp.einsum("tgrd,jgd->tgrj", query4, key_row, preferred_element_type=F32) * score_scale
    )
    scores = jnp.where(allowed, scores, NEG)
    row_max = jnp.max(scores, axis=-1)
    weights = jnp.where(allowed, jnp.exp(scores - row_max[..., None]), 0.0)
    row_sum = jnp.sum(weights, axis=-1)
    probs = weights / row_sum[..., None]
    probs_b = probs.astype(BF)
    accum = jnp.einsum("tgrj,jgd->tgrd", probs_b, value_row, preferred_element_type=F32)
    attn4 = accum.astype(BF)
    attn_b = attn4.reshape(tok_rows, H * HD)
    mixed = resid + dot(attn_b, wo)
    normed_mlp, inv_mlp = norm_forward(mixed, gain_mlp)
    normed_mlp_b = normed_mlp.astype(BF)
    gate = dot(normed_mlp_b, wg)
    upper = dot(normed_mlp_b, wu)
    sigma = jax.nn.sigmoid(gate)
    act_b = (gate * sigma * upper).astype(BF)
    result = (mixed + dot(act_b, wd)).astype(BF)

    grad_act = dot(grad_out, wd.T)
    grad_gate_b = (grad_act * upper * sigma * (1.0 + gate * (1.0 - sigma))).astype(BF)
    grad_up_b = (grad_act * gate * sigma).astype(BF)
    grad_normed_mlp = dot(grad_gate_b, wg.T) + dot(grad_up_b, wu.T)
    grad_mixed_n, grad_gain_mlp = norm_backward(mixed, inv_mlp, gain_mlp, grad_normed_mlp)
    grad_mixed = grad_out.astype(F32) + grad_mixed_n
    grad_mixed_b = grad_mixed.astype(BF)
    grad_attn_b = dot(grad_mixed_b, wo.T).astype(BF)
    grad_attn4 = grad_attn_b.reshape(tok_rows, KV, groups, HD)
    delta = jnp.sum(grad_attn4.astype(F32) * attn4.astype(F32), axis=-1)

    value_part = jnp.einsum("tgrj,tgrd->jgd", probs_b, grad_attn4, preferred_element_type=F32)
    grad_probs = jnp.einsum("tgrd,jgd->tgrj", grad_attn4, value_row, preferred_element_type=F32)
    grad_scores = (probs * (grad_probs - delta[..., None])).astype(BF)
    grad_query = (
        jnp.einsum("tgrj,jgd->tgrd", grad_scores, key_row, preferred_element_type=F32)
        * score_scale
    )
    key_part = (
        jnp.einsum("tgrj,tgrd->jgd", grad_scores, query4, preferred_element_type=F32)
        * score_scale
    )
    parts = jnp.concatenate(
        [key_part.reshape(row_len, KV * HD), value_part.reshape(row_len, KV * HD)], axis=1
    )
    _, (parts,) = exchange(n, 2, [], [parts.astype(BF).reshape(n, tok_rows, 2 * KV * HD)])
    own = jnp.sum(parts.astype(F32), axis=0)
    own_keys = own[:, : KV * HD].reshape(tok_rows, KV, HD)
    grad_query_b = (
        rotate(grad_query.reshape(tok_rows, H, HD), cos_table, sin_table, -1.0)
        .astype(BF)
        .reshape(tok_rows, H * HD)
    )
    grad_key_b = (
        rotate(own_keys, cos_table, sin_table, -1.0).astype(BF).reshape(tok_rows, KV * HD)
    )
    grad_value_b = own[:, KV * HD :].astype(BF)
    grad_qkv_b = jnp.concatenate([grad_query_b, grad_key_b, grad_value_b], axis=1)
    grad_normed = dot(grad_qkv_b, wqkv.T)
    grad_resid_n, grad_gain_attn = norm_backward(resid, inv_attn, gain_attn, grad_normed)
    grad_hidden = grad_mixed + grad_resid_n

    gain_parts = jnp.stack([grad_gain_attn, grad_gain_mlp]).reshape(2, n, rows)
    gain_parts = jnp.pad(gain_parts.transpose(1, 0, 2), ((0, 0), (0, 6), (0, 0)))

    def sliced(x):
        return x.reshape(tok_rows, n, -1).transpose(1, 0, 2)

    right_small = jnp.concatenate([grad_qkv_b, grad_mixed_b], axis=1)
    (g_gate, g_up, g_small, g_out), (x_attn, x_ctx, x_mlp, x_act, gain_parts) = exchange(
        n,
        3,
        [grad_gate_b, grad_up_b, right_small, grad_out],
        [sliced(normed_b), sliced(attn_b), sliced(normed_mlp_b), sliced(act_b), gain_parts],
    )

    def padded(x):
        size = x.shape[-1]
        full = -(-size // (16 * reps)) * (16 * reps)
        return jnp.pad(x.reshape(row_len, size), ((0, 0), (0, full - size)))

    def product(x, g):
        return dot(padded(x).T, g.reshape(row_len, -1)).astype(BF)

    g_small = g_small.reshape(row_len, -1)
    small = jnp.concatenate(
        [product(x_attn, g_small[:, :cut]), product(x_ctx, g_small[:, cut:])], axis=1
    )
    gain_own, (t_gate, t_up, t_small, t_down) = rep_sum(
        reps,
        4,
        jnp.sum(gain_parts, axis=0),
        [product(x_mlp, g_gate), product(x_mlp, g_up), small, product(x_act, g_out)],
    )
    t_small = t_small[:rows].astype(F32)
    return (
        result,
        grad_hidden,
        gain_own[0],
        t_small[:, :q],
        t_small[:, q : q + k],
        t_small[:, q + k : q + 2 * k],
        t_small[:, q + 2 * k :],
        gain_own[1],
        t_gate[:rows].astype(F32),
        t_up[:rows].astype(F32),
        t_down[: w_down.shape[0]].astype(F32),
    )


def solution(mesh):
    both = P(("rep", "shard"), None)
    tokens = P(("rep", "shard"))
    vector = P("shard")
    matrix = P("shard", None)
    return jax.shard_map(
        functools.partial(local, mesh.shape["shard"], mesh.shape["rep"]),
        mesh=mesh,
        in_specs=(both, tokens, tokens, vector, matrix, matrix, matrix, matrix, vector)
        + (matrix, matrix, matrix, both),
        out_specs=(both, both, vector, matrix, matrix, matrix, matrix, vector)
        + (matrix, matrix, matrix),
        check_vma=False,
    )
```

```python
import functools
import math

import jax
import jax.numpy as jnp
from jax import lax
from jax.experimental import pallas as pl
from jax.experimental.pallas import tpu as pltpu
from jax.sharding import PartitionSpec as P

H = 15
KV = 5
HD = 64

EPS = 1e-05
THETA = 100000.0
NEG = -1e30
MESH = pl.DeviceIdType.MESH
BF = jnp.bfloat16
F32 = jnp.float32


def rope_tables(positions, head_size):
    half_size = head_size // 2
    frequency = THETA ** (-(jnp.arange(half_size, dtype=F32) * 2.0 / head_size))
    angles = positions.astype(F32)[:, None] * frequency[None, :]
    return (jnp.cos(angles), jnp.sin(angles))


def rotate(values, cosine, sine, direction):
    half_size = values.shape[-1] // 2
    first_half = values[..., :half_size]
    second_half = values[..., half_size:]
    cos_table = cosine[:, None, :]
    sin_table = sine[:, None, :] * direction
    return jnp.concatenate(
        [
            first_half * cos_table - second_half * sin_table,
            second_half * cos_table + first_half * sin_table,
        ],
        axis=-1,
    )


def norm_forward(values, gain):
    inverse = lax.rsqrt(jnp.mean(values * values, axis=-1, keepdims=True) + EPS)
    return (values * inverse * gain, inverse)


def norm_backward(values, inverse, gain, upstream):
    scaled = upstream * gain
    grad_gain = jnp.sum(upstream * values * inverse, axis=0)
    inner = jnp.mean(scaled * values, axis=-1, keepdims=True)
    return (inverse * scaled - values * inverse * inverse * inverse * inner, grad_gain)


def dot(a, b):
    return jnp.dot(a, b, preferred_element_type=F32)


def exchange_kernel(n, n_gather, n_scatter, *refs):
    total = n_gather + n_scatter
    ins, outs, refs = refs[:total], refs[total : 2 * total], refs[2 * total :]
    held, (local_sem, send_sem, recv_sem) = refs[:total], refs[total:]
    me = lax.axis_index("shard")
    chips = n // 2
    chip, core = me // 2, me % 2
    mate = 2 * chip + (1 - core)

    barrier = pltpu.get_barrier_semaphore()
    for d in range(1, n):
        pl.semaphore_signal(
            barrier, inc=1, device_id={"shard": (me + d) % n}, device_id_type=MESH
        )
    pl.semaphore_wait(barrier, n - 1)

    count = [0]

    def remote(src, dst, to):
        i = count[0]
        count[0] += 1
        copy = pltpu.make_async_remote_copy(
            src_ref=src,
            dst_ref=dst,
            send_sem=send_sem.at[i],
            recv_sem=recv_sem.at[i],
            device_id={"shard": to},
            device_id_type=MESH,
        )
        copy.start()
        return copy

    pending = []
    far = []
    for a in range(n_gather):
        for k in range(1, chips):
            peer = 2 * ((chip + k) % chips) + core
            far.append((a, k, remote(ins[a], outs[a].at[me], peer)))
    for a in range(n_gather, total):
        for d in range(1, n):
            peer = (me + d) % n
            pending.append(remote(ins[a].at[peer], outs[a].at[me], peer))
    for a in range(n_gather):
        pending.append(remote(ins[a], outs[a].at[me], mate))
    own = []
    for a in range(total):
        src = ins[a] if a < n_gather else ins[a].at[me]
        copy = pltpu.make_async_copy(src, held[a], local_sem.at[a])
        copy.start()
        own.append(copy)
    for a in range(total):
        own[a].wait()
        own[a] = pltpu.make_async_copy(held[a], outs[a].at[me], local_sem.at[total + a])
        own[a].start()
    for a, k, copy in far:
        copy.wait_recv()
        origin = 2 * ((chip + chips - k) % chips) + core
        pending.append(remote(outs[a].at[origin], outs[a].at[origin], mate))
    for _, _, copy in far:
        copy.wait_send()
    for copy in pending:
        copy.wait()
    for copy in own:
        copy.wait()


def exchange(n, cid, gathers, scatters):
    chips = n // 2
    g, s = len(gathers), len(scatters)
    copies = g * (2 * (chips - 1) + 1) + s * (n - 1)
    shapes = [jax.ShapeDtypeStruct((n,) + a.shape, a.dtype) for a in gathers]
    shapes += [jax.ShapeDtypeStruct(a.shape, a.dtype) for a in scatters]
    out = pl.pallas_call(
        functools.partial(exchange_kernel, n, g, s),
        out_shape=shapes,
        in_specs=[pl.BlockSpec(memory_space=pl.ANY)] * (g + s),
        out_specs=[pl.BlockSpec(memory_space=pl.ANY)] * (g + s),
        scratch_shapes=[pltpu.VMEM(a.shape, a.dtype) for a in gathers]
        + [pltpu.VMEM(a.shape[1:], a.dtype) for a in scatters]
        + [
            pltpu.SemaphoreType.DMA((2 * (g + s),)),
            pltpu.SemaphoreType.DMA((copies,)),
            pltpu.SemaphoreType.DMA((copies,)),
        ],
        compiler_params=pltpu.CompilerParams(
            collective_id=cid, has_side_effects=True, vmem_limit_bytes=32 * 1024 * 1024
        ),
    )(*gathers, *scatters)
    return out[:g], out[g:]


def weight_kernel(n, n_small, axes, *refs):
    n_big = len(axes)
    total = n_small + n_big
    ins, outs, refs = refs[:total], refs[total : 2 * total], refs[2 * total :]
    held, (local_sem, send_sem, recv_sem) = refs[:total], refs[total:]
    me, rep = lax.axis_index("shard"), lax.axis_index("rep")
    chips = n // 2
    chip, core = me // 2, me % 2
    mate = {"shard": 2 * chip + (1 - core)}
    near_a = {"rep": rep + 1 - 2 * (rep % 2)}
    near_b = {"rep": rep + 2 - 4 * ((rep // 2) % 2)}
    own_q = rep % 4
    quarter_b, quarter_d = (own_q + 2) % 4, 3 - own_q
    quarter_a = own_q + 1 - 2 * (own_q % 2)

    barrier = pltpu.get_barrier_semaphore()
    for d in range(1, n):
        pl.semaphore_signal(
            barrier, inc=1, device_id={"shard": (me + d) % n}, device_id_type=MESH
        )
    for there in (near_a, near_b):
        pl.semaphore_signal(barrier, inc=1, device_id=there, device_id_type=MESH)
    pl.semaphore_wait(barrier, n + 1)

    count = [0]

    def remote(src, dst, to):
        i = count[0]
        count[0] += 1
        copy = pltpu.make_async_remote_copy(
            src_ref=src,
            dst_ref=dst,
            send_sem=send_sem.at[i],
            recv_sem=recv_sem.at[i],
            device_id=to,
            device_id_type=MESH,
        )
        copy.start()
        return copy

    def piece(ref, a, which, part=None):
        axis = axes[a - n_small]
        unit = 16 if axis == 0 else 128
        size = ins[a].shape[axis] // 4
        lo = (size // unit) * 2 // 5 * unit
        first, length = {None: (0, size), 0: (0, lo), 1: (lo, size - lo)}[part]
        at = pl.ds(pl.multiple_of(which * size + first, unit), length)
        return ref.at[at, :] if axis == 0 else ref.at[:, at]

    waits = []
    received = []

    def to_mate(ref):
        waits.append(remote(ref, ref, mate))

    def arrived(copy):
        copy.wait_recv()
        received.append(copy)

    direct, side_a, side_b, corner_x, corner_a, plain = {}, {}, {}, {}, {}, []
    for a in range(n_small):
        for k in range(1, chips):
            peer = {"shard": 2 * ((chip + k) % chips) + core}
            plain.append((a, k, remote(ins[a], outs[a].at[me], peer)))
        waits.append(remote(ins[a], outs[a].at[me], mate))

    def start_direct(a):
        for k in range(1, chips):
            peer = {"shard": 2 * ((chip + k) % chips) + core}
            direct[a, k] = remote(
                piece(ins[a], a, own_q), piece(outs[a].at[me], a, own_q), peer
            )

    def start_corner(a):
        for k in range(1, chips):
            peer = {"shard": 2 * ((chip + k) % chips) + core}
            corner_x[a, k] = remote(
                piece(ins[a], a, quarter_d, 0), piece(outs[a].at[me], a, quarter_d, 0), peer
            )

    start_direct(n_small)
    own = []
    for a in range(total):
        if a >= n_small:
            waits.append(remote(ins[a], outs[a].at[me], mate))
        copy = pltpu.make_async_copy(ins[a], held[a], local_sem.at[a])
        copy.start()
        own.append(copy)
    for a in range(total):
        own[a].wait()
        own[a] = pltpu.make_async_copy(held[a], outs[a].at[me], local_sem.at[total + a])
        own[a].start()

    def origin(k):
        return 2 * ((chip + chips - k) % chips) + core

    def spread(a):
        for k in range(1, chips):
            direct[a, k].wait()
        if a + 1 < total:
            start_direct(a + 1)
        else:
            for b in range(n_small, total):
                start_corner(b)
        for k in range(1, chips):
            block = piece(outs[a].at[origin(k)], a, own_q)
            side_a[a, k] = remote(block, block, near_a)
            side_b[a, k] = remote(block, block, near_b)
            to_mate(block)

    def pass_on(a):
        for k in range(1, chips):
            arrived(side_b[a, k])
            slot = outs[a].at[origin(k)]
            block = piece(slot, a, quarter_b, 1)
            corner_a[a, k] = remote(block, block, near_a)
            to_mate(piece(slot, a, quarter_b))
            arrived(side_a[a, k])
            to_mate(piece(slot, a, quarter_a))

    def finish(a):
        for k in range(1, chips):
            slot = outs[a].at[origin(k)]
            arrived(corner_x[a, k])
            to_mate(piece(slot, a, quarter_d, 0))
            arrived(corner_a[a, k])
            to_mate(piece(slot, a, quarter_d, 1))

    for t in range(n_big + 1):
        if t < n_big:
            spread(n_small + t)
        if 0 <= t - 1 < n_big:
            pass_on(n_small + t - 1)
    for a in range(n_small, total):
        finish(a)
    for a, k, copy in plain:
        arrived(copy)
        to_mate(outs[a].at[origin(k)])
    for copy in received:
        copy.wait_send()
    for copy in waits:
        copy.wait()
    for copy in own:
        copy.wait()


def gather_weights(n, cid, small, big):
    arrays = list(small) + [a for a, _ in big]
    chips = n // 2
    copies = len(small) * (2 * chips - 1) + len(big) * (10 * (chips - 1) + 1)
    total = len(arrays)
    return pl.pallas_call(
        functools.partial(weight_kernel, n, len(small), tuple(axis for _, axis in big)),
        out_shape=[jax.ShapeDtypeStruct((n,) + a.shape, a.dtype) for a in arrays],
        in_specs=[pl.BlockSpec(memory_space=pl.ANY)] * total,
        out_specs=[pl.BlockSpec(memory_space=pl.ANY)] * total,
        scratch_shapes=[pltpu.VMEM(a.shape, a.dtype) for a in arrays]
        + [
            pltpu.SemaphoreType.DMA((2 * total,)),
            pltpu.SemaphoreType.DMA((copies,)),
            pltpu.SemaphoreType.DMA((copies,)),
        ],
        compiler_params=pltpu.CompilerParams(
            collective_id=cid, has_side_effects=True, vmem_limit_bytes=32 * 1024 * 1024
        ),
    )(*arrays)


def rep_sum_kernel(zs, n, *refs):
    gain_in, refs = refs[0], refs[1:]
    ins, gain_out, refs = refs[:n], refs[n], refs[n + 1 :]
    outs, near, sums = refs[:n], refs[n : 2 * n], refs[2 * n : 3 * n]
    others = refs[3 * n : 4 * n]
    gain_near, gain_pair, gain_all, send_sem, recv_sem = refs[4 * n :]
    me = lax.axis_index("rep")
    side, place = me % 2, me // 2
    partner = 2 * place + (1 - side)

    barrier = pltpu.get_barrier_semaphore()
    pl.semaphore_signal(barrier, inc=1, device_id={"rep": partner}, device_id_type=MESH)
    for k in range(1, zs):
        peer = 2 * ((place + k) % zs) + side
        pl.semaphore_signal(barrier, inc=1, device_id={"rep": peer}, device_id_type=MESH)
    pl.semaphore_wait(barrier, zs)

    count = [0]

    def remote(src, dst, to):
        i = count[0]
        count[0] += 1
        copy = pltpu.make_async_remote_copy(
            src_ref=src,
            dst_ref=dst,
            send_sem=send_sem.at[i],
            recv_sem=recv_sem.at[i],
            device_id={"rep": to},
            device_id_type=MESH,
        )
        copy.start()
        return copy

    gain_first = remote(gain_in, gain_near, partner)
    first = [remote(ins[0].at[1 - side], near[0], partner)]
    second, third, fourth = {}, {}, {}
    gain_first.wait_recv()
    gain_pair[...] = gain_in[...] + gain_near[...]
    gain_all[place] = gain_pair[...]
    gain_second = [
        remote(gain_pair, gain_all.at[place], 2 * ((place + k) % zs) + side)
        for k in range(1, zs)
    ]

    def pair_sum(a):
        first[a].wait()
        if a + 1 < n:
            first.append(remote(ins[a + 1].at[1 - side], near[a + 1], partner))

        def body(z, carry):
            sums[a][z] = (ins[a][side, z].astype(F32) + near[a][z].astype(F32)).astype(BF)
            return carry

        lax.fori_loop(0, zs, body, 0)
        second[a] = []
        for k in range(1, zs):
            at = (place + k) % zs
            second[a].append(remote(sums[a].at[at], others[a].at[k - 1], 2 * at + side))

    def line_sum(a):
        for copy in second[a]:
            copy.wait_recv()
        value = sums[a][place].astype(F32)
        for k in range(1, zs):
            value = value + others[a][k - 1].astype(F32)
        outs[a][side, place] = value.astype(BF)
        third[a] = []
        for k in range(1, zs):
            at = (place + k) % zs
            block = outs[a].at[side, place]
            third[a].append(remote(block, block, 2 * at + side))

    def share(a):
        for copy in third[a]:
            copy.wait_recv()
        fourth[a] = remote(outs[a].at[side], outs[a].at[side], partner)

    for t in range(n + 2):
        if t < n:
            pair_sum(t)
        if 0 <= t - 1 < n:
            line_sum(t - 1)
        if 0 <= t - 2 < n:
            share(t - 2)
    for copy in gain_second:
        copy.wait()
    value = gain_all[0]
    for z in range(1, zs):
        value = value + gain_all[z]
    gain_out[...] = value
    gain_first.wait_send()
    for a in range(n):
        for copy in second[a]:
            copy.wait_send()
        for copy in third[a]:
            copy.wait_send()
        fourth[a].wait()


def rep_sum(reps, cid, gain, arrays):
    zs = reps // 2
    n = len(arrays)
    blocks = [a.reshape(2, zs, a.shape[0] // reps, a.shape[1]) for a in arrays]
    copies = n * (2 + 2 * (zs - 1)) + zs
    out = pl.pallas_call(
        functools.partial(rep_sum_kernel, zs, n),
        out_shape=[jax.ShapeDtypeStruct(b.shape, b.dtype) for b in [gain] + blocks],
        in_specs=[pl.BlockSpec(memory_space=pltpu.VMEM)] * (n + 1),
        out_specs=[pl.BlockSpec(memory_space=pltpu.VMEM)] * (n + 1),
        scratch_shapes=[pltpu.VMEM(b.shape[1:], BF) for b in blocks]
        + [pltpu.VMEM(b.shape[1:], BF) for b in blocks]
        + [pltpu.VMEM((zs - 1,) + b.shape[2:], BF) for b in blocks]
        + [pltpu.VMEM(gain.shape, F32)] * 2
        + [pltpu.VMEM((zs,) + gain.shape, F32)]
        + [pltpu.SemaphoreType.DMA((copies,)), pltpu.SemaphoreType.DMA((copies,))],
        compiler_params=pltpu.CompilerParams(
            collective_id=cid, has_side_effects=True, vmem_limit_bytes=44 * 1024 * 1024
        ),
    )(gain, *blocks)
    return out[0], [o.reshape(a.shape) for o, a in zip(out[1:], arrays)]


def local(
    n,
    reps,
    hidden_in,
    segment_ids,
    positions,
    norm_attn,
    w_query,
    w_key,
    w_value,
    w_out,
    norm_mlp,
    w_gate,
    w_up,
    w_down,
    grad_out,
):
    tok_rows, width = hidden_in.shape
    row_len = tok_rows * n
    first_row = lax.axis_index("shard") * tok_rows
    groups = H // KV
    score_scale = 1.0 / math.sqrt(HD)
    query_idx = first_row + jnp.arange(tok_rows, dtype=jnp.int32)

    gains = jnp.pad(jnp.stack([norm_attn, norm_mlp]), ((0, 14), (0, 0)))
    seg8 = jnp.broadcast_to(segment_ids[None, :], (8, tok_rows))
    rows = width // n

    def row_pad(x, unit):
        return jnp.pad(x, ((0, -x.shape[0] % unit), (0, 0)))

    w_small = jnp.concatenate([w_query, w_key, w_value, w_out], axis=1)
    got = gather_weights(
        n,
        0,
        [seg8, gains],
        [
            (row_pad(w_small, 16), 1),
            (row_pad(w_gate, 16), 1),
            (row_pad(w_up, 16), 1),
            (row_pad(w_down, 64), 0),
        ],
    )
    row_segments = got[0][:, 0, :].reshape(row_len)
    gain_attn = got[1][:, 0, :].reshape(width).astype(F32)
    gain_mlp = got[1][:, 1, :].reshape(width).astype(F32)
    ws, wg, wu = [w[:, :rows].reshape(width, -1) for w in got[2:5]]
    wd = got[5][:, : w_down.shape[0]].reshape(-1, width)
    q, k = H * HD, KV * HD
    cut = q + 2 * k
    wqkv, wo = ws[:, :cut], ws[:, cut:]

    key_idx = jnp.arange(row_len, dtype=jnp.int32)
    allowed = (
        (segment_ids[:, None] == row_segments[None, :])
        & (key_idx[None, :] <= query_idx[:, None])
    )[:, None, None, :]

    resid = hidden_in.astype(F32)
    normed, inv_attn = norm_forward(resid, gain_attn)
    normed_b = normed.astype(BF)
    cos_table, sin_table = rope_tables(positions, HD)
    qkv = dot(normed_b, wqkv)
    query = qkv[:, :q].reshape(tok_rows, H, HD)
    query_b = rotate(query, cos_table, sin_table, 1.0).astype(BF)
    keys = qkv[:, q : q + k].reshape(tok_rows, KV, HD)
    key_b = rotate(keys, cos_table, sin_table, 1.0).astype(BF)
    value_b = qkv[:, q + k :].astype(BF)
    query4 = query_b.reshape(tok_rows, KV, groups, HD)
    (kv_row,), _ = exchange(
        n, 1, [jnp.concatenate([key_b.reshape(tok_rows, KV * HD), value_b], axis=1)], []
    )
    kv_row = kv_row.reshape(row_len, 2, KV, HD)
    key_row, value_row = kv_row[:, 0], kv_row[:, 1]

    scores = (
        jnp.einsum("tgrd,jgd->tgrj", query4, key_row, preferred_element_type=F32) * score_scale
    )
    scores = jnp.where(allowed, scores, NEG)
    row_max = jnp.max(scores, axis=-1)
    weights = jnp.where(allowed, jnp.exp(scores - row_max[..., None]), 0.0)
    row_sum = jnp.sum(weights, axis=-1)
    probs = weights / row_sum[..., None]
    probs_b = probs.astype(BF)
    accum = jnp.einsum("tgrj,jgd->tgrd", probs_b, value_row, preferred_element_type=F32)
    attn4 = accum.astype(BF)
    attn_b = attn4.reshape(tok_rows, H * HD)
    mixed = resid + dot(attn_b, wo)
    normed_mlp, inv_mlp = norm_forward(mixed, gain_mlp)
    normed_mlp_b = normed_mlp.astype(BF)
    gate = dot(normed_mlp_b, wg)
    upper = dot(normed_mlp_b, wu)
    sigma = jax.nn.sigmoid(gate)
    act_b = (gate * sigma * upper).astype(BF)
    result = (mixed + dot(act_b, wd)).astype(BF)

    grad_act = dot(grad_out, wd.T)
    grad_gate_b = (grad_act * upper * sigma * (1.0 + gate * (1.0 - sigma))).astype(BF)
    grad_up_b = (grad_act * gate * sigma).astype(BF)
    grad_normed_mlp = dot(grad_gate_b, wg.T) + dot(grad_up_b, wu.T)
    grad_mixed_n, grad_gain_mlp = norm_backward(mixed, inv_mlp, gain_mlp, grad_normed_mlp)
    grad_mixed = grad_out.astype(F32) + grad_mixed_n
    grad_mixed_b = grad_mixed.astype(BF)
    grad_attn_b = dot(grad_mixed_b, wo.T).astype(BF)
    grad_attn4 = grad_attn_b.reshape(tok_rows, KV, groups, HD)
    delta = jnp.sum(grad_attn4.astype(F32) * attn4.astype(F32), axis=-1)

    value_part = jnp.einsum("tgrj,tgrd->jgd", probs_b, grad_attn4, preferred_element_type=F32)
    grad_probs = jnp.einsum("tgrd,jgd->tgrj", grad_attn4, value_row, preferred_element_type=F32)
    grad_scores = (probs * (grad_probs - delta[..., None])).astype(BF)
    grad_query = (
        jnp.einsum("tgrj,jgd->tgrd", grad_scores, key_row, preferred_element_type=F32)
        * score_scale
    )
    key_part = (
        jnp.einsum("tgrj,tgrd->jgd", grad_scores, query4, preferred_element_type=F32)
        * score_scale
    )
    parts = jnp.concatenate(
        [key_part.reshape(row_len, KV * HD), value_part.reshape(row_len, KV * HD)], axis=1
    )
    _, (parts,) = exchange(n, 2, [], [parts.astype(BF).reshape(n, tok_rows, 2 * KV * HD)])
    own = jnp.sum(parts.astype(F32), axis=0)
    own_keys = own[:, : KV * HD].reshape(tok_rows, KV, HD)
    grad_query_b = (
        rotate(grad_query.reshape(tok_rows, H, HD), cos_table, sin_table, -1.0)
        .astype(BF)
        .reshape(tok_rows, H * HD)
    )
    grad_key_b = (
        rotate(own_keys, cos_table, sin_table, -1.0).astype(BF).reshape(tok_rows, KV * HD)
    )
    grad_value_b = own[:, KV * HD :].astype(BF)
    grad_qkv_b = jnp.concatenate([grad_query_b, grad_key_b, grad_value_b], axis=1)
    grad_normed = dot(grad_qkv_b, wqkv.T)
    grad_resid_n, grad_gain_attn = norm_backward(resid, inv_attn, gain_attn, grad_normed)
    grad_hidden = grad_mixed + grad_resid_n

    gain_parts = jnp.stack([grad_gain_attn, grad_gain_mlp]).reshape(2, n, rows)
    gain_parts = jnp.pad(gain_parts.transpose(1, 0, 2), ((0, 0), (0, 6), (0, 0)))

    def sliced(x):
        return x.reshape(tok_rows, n, -1).transpose(1, 0, 2)

    right_small = jnp.concatenate([grad_qkv_b, grad_mixed_b], axis=1)
    (g_gate, g_up, g_small, g_out), (x_attn, x_ctx, x_mlp, x_act, gain_parts) = exchange(
        n,
        3,
        [grad_gate_b, grad_up_b, right_small, grad_out],
        [sliced(normed_b), sliced(attn_b), sliced(normed_mlp_b), sliced(act_b), gain_parts],
    )

    def padded(x):
        size = x.shape[-1]
        full = -(-size // (16 * reps)) * (16 * reps)
        return jnp.pad(x.reshape(row_len, size), ((0, 0), (0, full - size)))

    def product(x, g):
        return dot(padded(x).T, g.reshape(row_len, -1)).astype(BF)

    g_small = g_small.reshape(row_len, -1)
    small = jnp.concatenate(
        [product(x_attn, g_small[:, :cut]), product(x_ctx, g_small[:, cut:])], axis=1
    )
    gain_own, (t_gate, t_up, t_small, t_down) = rep_sum(
        reps,
        4,
        jnp.sum(gain_parts, axis=0),
        [product(x_mlp, g_gate), product(x_mlp, g_up), small, product(x_act, g_out)],
    )
    t_small = t_small[:rows].astype(F32)
    return (
        result,
        grad_hidden,
        gain_own[0],
        t_small[:, :q],
        t_small[:, q : q + k],
        t_small[:, q + k : q + 2 * k],
        t_small[:, q + 2 * k :],
        gain_own[1],
        t_gate[:rows].astype(F32),
        t_up[:rows].astype(F32),
        t_down[: w_down.shape[0]].astype(F32),
    )


def solution(mesh):
    both = P(("rep", "shard"), None)
    tokens = P(("rep", "shard"))
    vector = P("shard")
    matrix = P("shard", None)
    return jax.shard_map(
        functools.partial(local, mesh.shape["shard"], mesh.shape["rep"]),
        mesh=mesh,
        in_specs=(both, tokens, tokens, vector, matrix, matrix, matrix, matrix, vector)
        + (matrix, matrix, matrix, both),
        out_specs=(both, both, vector, matrix, matrix, matrix, matrix, vector)
        + (matrix, matrix, matrix),
        check_vma=False,
    )
```
